32 devices in a mesh: seq: 8 (over z, x), grp: 4 (over y, core).
Axes of the slice: x: 2, y: 2, z: 4, core: 2. Of those that a mesh axis runs over, the one named last changes fastest.
Arguments:
- query_proj: bfloat16 [2048, 4096], P('seq', 'grp'), may hold values from -6 to 6
- key_proj: bfloat16 [2048, 4096], P('seq', 'grp'), may hold values from -6 to 6
- value_proj: bfloat16 [2048, 4096], P('seq', 'grp'), may hold values from -6 to 6
- out_grad: bfloat16 [2048, 4096], P('seq', 'grp'), may hold values from -22 to 22
- filters: bfloat16 [256, 128], P('grp'), may hold values from -0.5 to 0.5
Outputs:
- query_grad: bfloat16 [2048, 4096], P('seq', 'grp')
- key_grad: bfloat16 [2048, 4096], P('seq', 'grp')
- value_grad: bfloat16 [2048, 4096], P('seq', 'grp')
- filter_grad: float32 [256, 128], P('grp')
The draws below stay inside these ranges and needn't reach their ends.
All inputs are finite; a program needn't handle non-finite values.
Results may differ from the reference program's by a relative error of at most 0.005.
Values may be sent and summed in bfloat16 or wider, within the bound.
A program may use at most 64 MiB of HBM per device.

```python
import jax
import jax.numpy as jnp
from jax import lax

D = 4096
GSIZE = 16
K = 128
TOKENS = 2048
GROUPS = 256


def draw_out_grad(key, part):
    first = jax.random.fold_in(jax.random.fold_in(key, 7), 0)
    token_pos = jnp.arange(TOKENS, dtype=jnp.float32)[:, None] / TOKENS
    chan_pos = jnp.arange(D, dtype=jnp.float32)[None, :] / D
    base = jnp.clip(jax.random.normal(first, (TOKENS, D), jnp.float32), -4.0, 4.0)
    scale = 10.0 ** (chan_pos - 0.5) * 3.0 ** (token_pos - 0.5)
    return jnp.clip(base * scale, -22.0, 22.0).astype(jnp.bfloat16)


def level_of(key, dims, cuts, low, high):
    gain = 1.0
    for axis_at, parts in cuts:
        heights = jax.random.uniform(jax.random.fold_in(jax.random.fold_in(key, 6), axis_at), (parts,), jnp.float32, low / len(cuts), high / len(cuts))
        gain = gain * jnp.repeat(jnp.exp(heights), dims[axis_at] // parts).reshape((-1,) + (1,) * (len(dims) - 1 - axis_at))
    return gain


def centred(stream_key, shape, width, reach, pieces=(), held_as=jnp.bfloat16):
    values = width * jax.random.normal(stream_key, shape, jnp.float32)
    if pieces:
        values = values * level_of(stream_key, shape, pieces, -0.22, 0.18)
    return jnp.clip(values, -reach, reach).astype(held_as)


def setup_inputs(seed: int = 0) -> dict:
    splits = jax.random.split(jax.random.key(seed), 6)
    query_proj = centred(splits[0], (TOKENS, D), 1.0, 6.0, ((0, 8), (1, 4)))
    key_proj = centred(splits[1], (TOKENS, D), 1.0, 6.0, ((0, 8), (1, 4)))
    value_proj = centred(splits[2], (TOKENS, D), 1.0, 6.0, ((0, 8), (1, 4)))
    out_grad = draw_out_grad(jax.random.fold_in(splits[5], 71), 0)
    filters = centred(splits[4], (GROUPS, K), K ** -0.5, 0.5, ((0, 4),))
    return {"query_proj": query_proj, "key_proj": key_proj, "value_proj": value_proj, "out_grad": out_grad, "filters": filters}


def forward_table(filt):
    group_n, tap_count = filt.shape
    return jnp.concatenate([jnp.zeros((group_n, 1), filt.dtype), jnp.flip(filt, axis=1), jnp.zeros((group_n, 2 * tap_count - 1), filt.dtype)], axis=1)

def backward_table(filt):
    group_n, tap_count = filt.shape
    return jnp.concatenate([filt, jnp.zeros((group_n, 2 * tap_count), filt.dtype)], axis=1)

def toeplitz(table):
    group_n, span_all = table.shape
    tap_count = span_all // 3
    tiled_rows = jnp.tile(table, (1, tap_count))
    return tiled_rows[:, :tap_count * (span_all - 1)].reshape(group_n, tap_count, span_all - 1)[:, :, :2 * tap_count]

def diagonal_sums(matrix):
    group_n, tap_count, span_two = matrix.shape
    flat_rows = matrix.reshape(group_n, tap_count * span_two)
    padded = jnp.pad(flat_rows, ((0, 0), (0, tap_count)))
    skewed = padded.reshape(group_n, tap_count, span_two + 1)[:, :, 1:tap_count + 1]
    return jnp.flip(lax.optimization_barrier(jnp.sum(skewed, axis=1)), axis=1)

def paired(blocks):
    return jnp.concatenate([blocks[:-1], blocks[1:]], axis=1)

def slab_grads(query, keyv, value, grad, filt):
    rows_all, cols_all = query.shape
    tap_count = filt.shape[1]
    block_count = rows_all // tap_count
    group_n = cols_all // GSIZE
    prod_u = (keyv.astype(jnp.float32) * value.astype(jnp.float32)).astype(jnp.bfloat16)
    prod_dz = (grad.astype(jnp.float32) * query.astype(jnp.float32)).astype(jnp.bfloat16)
    zero_rows = jnp.zeros((tap_count, cols_all), jnp.bfloat16)
    extended_in = jnp.concatenate([zero_rows, prod_u], axis=0).reshape(block_count + 1, tap_count, group_n, GSIZE).astype(jnp.float32)
    extended_dz = jnp.concatenate([prod_dz, zero_rows], axis=0).reshape(block_count + 1, tap_count, group_n, GSIZE).astype(jnp.float32)
    forward_mat = toeplitz(forward_table(filt)).astype(jnp.float32)
    backward_mat = toeplitz(backward_table(filt)).astype(jnp.float32)
    pairs_in = paired(extended_in)
    conv_out = jnp.einsum('gij,bjgc->bigc', forward_mat, pairs_in, precision=lax.Precision.HIGHEST).reshape(rows_all, cols_all)
    query_grad = (grad.astype(jnp.float32) * conv_out).astype(jnp.bfloat16)
    grad_in = jnp.einsum('gij,bjgc->bigc', backward_mat, paired(extended_dz), precision=lax.Precision.HIGHEST).reshape(rows_all, cols_all)
    key_grad = (grad_in * value.astype(jnp.float32)).astype(jnp.bfloat16)
    value_grad = (grad_in * keyv.astype(jnp.float32)).astype(jnp.bfloat16)
    corr = jnp.einsum('bigc,bjgc->gij', extended_dz[:-1], pairs_in, precision=lax.Precision.HIGHEST)
    raw_sums = diagonal_sums(corr)
    return (query_grad, key_grad, value_grad, raw_sums)

def reference(query_proj, key_proj, value_proj, out_grad, filters):
    slab_cols = 16 * GSIZE
    pieces_q, pieces_k, pieces_v, pieces_h = ([], [], [], [])
    for index in range(D // slab_cols):
        lo_col = index * slab_cols
        hi_col = lo_col + slab_cols
        filt = filters[index * 16:(index + 1) * 16]
        result = slab_grads(query_proj[:, lo_col:hi_col], key_proj[:, lo_col:hi_col], value_proj[:, lo_col:hi_col], out_grad[:, lo_col:hi_col], filt)
        pieces_q.append(result[0])
        pieces_k.append(result[1])
        pieces_v.append(result[2])
        pieces_h.append(result[3])
    raw_sums = jnp.concatenate(pieces_h, axis=0)
    squares = jnp.sum(raw_sums * raw_sums)
    factor = jnp.minimum(jnp.float32(1.0), jnp.sqrt(jnp.float32(GROUPS * K) / squares))
    filter_grad = raw_sums * factor
    return (jnp.concatenate(pieces_q, axis=1), jnp.concatenate(pieces_k, axis=1), jnp.concatenate(pieces_v, axis=1), filter_grad)
```

```python
import functools

import jax
import jax.numpy as jnp
from jax import lax
from jax.experimental import pallas as pl
from jax.experimental.pallas import tpu as pltpu
from jax.sharding import PartitionSpec as P

GSIZE = 16
LANES = 128
PER_TILE = LANES // GSIZE
MESH = pl.DeviceIdType.MESH
F32 = jnp.float32
BF16 = jnp.bfloat16


def product(a, b):
    return (a.astype(F32) * b.astype(F32)).astype(BF16)


def kernel(
    seq_n, grp_n, whole_sum, chunk_n,
    q_hbm, k_hbm, v_hbm, g_hbm, h_ref,
    qg_hbm, kg_hbm, vg_hbm, fg_ref,
    q, k, v, g, u, dz, u_halo, dz_halo, fmat, bmat, out_q, out_k, out_v,
    taps, raw, scattered, gathered, squares,
    in_sem, out_sem, halo_send, halo_recv, rs_send, rs_recv, ag_send, ag_recv, ss_send, ss_recv,
):
    me, mine = lax.axis_index("seq"), lax.axis_index("grp")
    tile_n = u.shape[0]
    half = LANES
    top, low = pl.ds(0, half), pl.ds(half, half)
    per_chunk = tile_n // chunk_n

    loads = []
    order = ((g_hbm, g, top), (q_hbm, q, top), (k_hbm, k, low), (v_hbm, v, low),
             (g_hbm, g, low), (q_hbm, q, low), (k_hbm, k, top), (v_hbm, v, top))
    for index, (source, target, rows) in enumerate(order):
        copy = pltpu.make_async_copy(source.at[rows], target.at[rows], in_sem.at[index])
        copy.start()
        loads.append(copy)

    def at_seq(position):
        return {"seq": position, "grp": mine}

    def at_grp(position):
        return {"seq": me, "grp": position}

    seq_peers = [lax.rem(me + step, seq_n) for step in range(1, seq_n)] if whole_sum else []
    grp_peers = [lax.rem(mine + step, grp_n) for step in range(1, grp_n)] if whole_sum else []
    has_left, has_right = me > 0, me < seq_n - 1
    barrier = pltpu.get_barrier_semaphore()
    if whole_sum:
        for peer in seq_peers:
            pl.semaphore_signal(barrier, 1, device_id=at_seq(peer), device_id_type=MESH)
        for peer in grp_peers:
            pl.semaphore_signal(barrier, 1, device_id=at_grp(peer), device_id_type=MESH)
    else:
        @pl.when(has_left)
        def _():
            pl.semaphore_signal(barrier, 1, device_id=at_seq(me - 1), device_id_type=MESH)

        @pl.when(has_right)
        def _():
            pl.semaphore_signal(barrier, 1, device_id=at_seq(me + 1), device_id_type=MESH)

    h = h_ref[...]
    row = lax.broadcasted_iota(jnp.int32, (half, half), 0)
    col = lax.broadcasted_iota(jnp.int32, (half, half), 1)
    flip = (((row + col) == 0) | ((row + col) == half)).astype(BF16)
    taps[0] = h.astype(F32)
    taps[1] = jnp.dot(h, flip, preferred_element_type=F32)

    @pl.when(jnp.logical_not(has_left))
    def _():
        u_halo[...] = jnp.zeros_like(u_halo)

    @pl.when(jnp.logical_not(has_right))
    def _():
        dz_halo[...] = jnp.zeros_like(dz_halo)

    def cols(tile):
        return pl.ds(pl.multiple_of(tile * LANES, LANES), LANES)

    def dz_copy(chunk):
        tiles = pl.ds(chunk * per_chunk, per_chunk)
        return pltpu.make_async_remote_copy(
            src_ref=dz.at[tiles, top], dst_ref=dz_halo.at[tiles],
            send_sem=halo_send.at[0, chunk], recv_sem=halo_recv.at[0, chunk],
            device_id=at_seq(me - 1), device_id_type=MESH)

    def u_copy(chunk):
        tiles = pl.ds(chunk * per_chunk, per_chunk)
        return pltpu.make_async_remote_copy(
            src_ref=u.at[tiles, low], dst_ref=u_halo.at[tiles],
            send_sem=halo_send.at[1, chunk], recv_sem=halo_recv.at[1, chunk],
            device_id=at_seq(me + 1), device_id_type=MESH)

    loads[0].wait()
    loads[1].wait()
    for tile in range(tile_n):
        dz[tile, top] = product(g[top, cols(tile)], q[top, cols(tile)])
    loads[2].wait()
    loads[3].wait()
    for tile in range(tile_n):
        u[tile, low] = product(k[low, cols(tile)], v[low, cols(tile)])

    if whole_sum:
        pl.semaphore_wait(barrier, seq_n + grp_n - 2)
    else:
        @pl.when(has_left)
        def _():
            pl.semaphore_wait(barrier, 1)

        @pl.when(has_right)
        def _():
            pl.semaphore_wait(barrier, 1)

    @pl.when(has_left)
    def _():
        for chunk in range(chunk_n):
            dz_copy(chunk).start()

    @pl.when(has_right)
    def _():
        for chunk in range(chunk_n):
            u_copy(chunk).start()

    for index in range(4, 8):
        loads[index].wait()
    for tile in range(tile_n):
        dz[tile, low] = product(g[low, cols(tile)], q[low, cols(tile)])
        u[tile, top] = product(k[top, cols(tile)], v[top, cols(tile)])

    lane_group = lax.broadcasted_iota(jnp.int32, (half, LANES), 1) // GSIZE

    def pick(stacked):
        out = stacked[0:half]
        for member in range(1, PER_TILE):
            out = jnp.where(lane_group == member, stacked[member * half:(member + 1) * half], out)
        return out

    def conv(table, tile, pair):
        return pick(jnp.dot(table[tile], pair, preferred_element_type=F32))

    def store_q(tile, rows, z):
        out_q[rows, cols(tile)] = (g[rows, cols(tile)].astype(F32) * z).astype(BF16)

    def store_kv(tile, rows, du):
        out_k[rows, cols(tile)] = (v[rows, cols(tile)].astype(F32) * du).astype(BF16)
        out_v[rows, cols(tile)] = (k[rows, cols(tile)].astype(F32) * du).astype(BF16)

    def local_part(tile, carry):
        base = pl.multiple_of(tile * PER_TILE, PER_TILE)
        plain = taps[0, pl.ds(base, PER_TILE), :]
        turned = taps[1, pl.ds(base, PER_TILE), :]
        for member in range(PER_TILE):
            rows = pl.ds(member * half, half)
            spread = jnp.broadcast_to(plain[member:member + 1], (half, half))
            circ = pltpu.roll(spread, 0, 1, stride=1, stride_axis=0)
            bmat[tile, rows, 0:half] = jnp.where(col >= row, circ, 0.0).astype(BF16)
            bmat[tile, rows, half:2 * half] = jnp.where(col < row, circ, 0.0).astype(BF16)
            spread = jnp.broadcast_to(turned[member:member + 1], (half, half))
            circ = pltpu.roll(spread, 0, 1, stride=1, stride_axis=0)
            fmat[tile, rows, 0:half] = jnp.where(col > row, circ, 0.0).astype(BF16)
            fmat[tile, rows, half:2 * half] = jnp.where(col <= row, circ, 0.0).astype(BF16)
        store_q(tile, low, conv(fmat, tile, u[tile]))
        store_kv(tile, top, conv(bmat, tile, dz[tile]))
        return carry

    lax.fori_loop(0, tile_n, local_part, 0)

    out_copies = []

    def send_out(source, target, rows):
        copy = pltpu.make_async_copy(source.at[rows], target.at[rows], out_sem.at[len(out_copies)])
        copy.start()
        out_copies.append(copy)

    send_out(out_q, qg_hbm, low)
    send_out(out_k, kg_hbm, top)
    send_out(out_v, vg_hbm, top)

    sub = lax.broadcasted_iota(jnp.int32, (PER_TILE, 8, LANES), 1)
    lanes256 = lax.broadcasted_iota(jnp.int32, (half, 2 * LANES), 1) % LANES // GSIZE

    def correlate(tile, carry):
        both = jnp.concatenate([u[tile, top], u[tile, low]], axis=1)
        window = jnp.concatenate(
            [jnp.concatenate([dz[tile, top], dz[tile, low]], axis=1),
             jnp.concatenate([dz[tile, low], dz_halo[tile]], axis=1)], axis=0)
        parts = []
        for member in range(PER_TILE):
            left = jnp.where(lanes256 == member, both, jnp.zeros_like(both))
            c = lax.dot_general(left, window, (((1,), (1,)), ((), ())), preferred_element_type=F32)
            m = jnp.where(col >= row, c[:, :half], c[:, half:])
            size = half // 2
            while size >= 8:
                m = m[:size] + pltpu.roll(m[size:], LANES - size, 1)
                size //= 2
            parts.append(m.reshape(1, 8, LANES))
        folded = jnp.concatenate(parts, axis=0)
        for bit in (1, 2, 4):
            folded = jnp.where((sub & bit) != 0, pltpu.roll(folded, LANES - bit, 2), folded)
        raw[pl.ds(pl.multiple_of(tile * PER_TILE, PER_TILE), PER_TILE), :] = jnp.sum(folded, axis=1)
        return carry

    for chunk in range(chunk_n):
        @pl.when(has_right)
        def _():
            dz_copy(chunk).wait_recv()

        lax.fori_loop(chunk * per_chunk, (chunk + 1) * per_chunk, correlate, 0)

    if whole_sum:
        own = raw.shape[0] // seq_n
        my_rows = pl.ds(pl.multiple_of(me * own, own), own)
        rs_copies, ag_copies, ss_copies = [], [], []
        for step, peer in enumerate(seq_peers):
            rs_copies.append(pltpu.make_async_remote_copy(
                src_ref=raw.at[pl.ds(pl.multiple_of(peer * own, own), own)],
                dst_ref=scattered.at[step], send_sem=rs_send.at[step], recv_sem=rs_recv.at[step],
                device_id=at_seq(peer), device_id_type=MESH))
            rs_copies[-1].start()
    else:
        fg_ref[...] = raw[...]

    def halo_q(tile, carry):
        pair = jnp.concatenate([u_halo[tile], u[tile, top]], axis=0)
        store_q(tile, top, conv(fmat, tile, pair))
        return carry

    def halo_kv(tile, carry):
        pair = jnp.concatenate([dz[tile, low], dz_halo[tile]], axis=0)
        store_kv(tile, low, conv(bmat, tile, pair))
        return carry

    lax.fori_loop(0, tile_n, halo_kv, 0)
    send_out(out_k, kg_hbm, low)
    send_out(out_v, vg_hbm, low)

    if whole_sum:
        total = raw[my_rows]
        for step, copy in enumerate(rs_copies):
            copy.wait_recv()
            total = total + scattered[step]
        gathered[my_rows] = total
        for step, peer in enumerate(seq_peers):
            ag_copies.append(pltpu.make_async_remote_copy(
                src_ref=gathered.at[my_rows], dst_ref=gathered.at[my_rows],
                send_sem=ag_send.at[step], recv_sem=ag_recv.at[step],
                device_id=at_seq(peer), device_id_type=MESH))
            ag_copies[-1].start()

    first = max(1, chunk_n // 2)
    for chunk in range(first):
        @pl.when(has_left)
        def _():
            u_copy(chunk).wait_recv()

    lax.fori_loop(0, first * per_chunk, halo_q, 0)

    if whole_sum:
        for copy in ag_copies:
            copy.wait_recv()
        values = gathered[...]
        part = jnp.sum((values * values).reshape(-1, 8, LANES), axis=0)
        squares[0] = part
        for step, peer in enumerate(grp_peers):
            ss_copies.append(pltpu.make_async_remote_copy(
                src_ref=squares.at[0], dst_ref=squares.at[step + 1],
                send_sem=ss_send.at[step], recv_sem=ss_recv.at[step],
                device_id=at_grp(peer), device_id_type=MESH))
            ss_copies[-1].start()

    for chunk in range(first, chunk_n):
        @pl.when(has_left)
        def _():
            u_copy(chunk).wait_recv()

    lax.fori_loop(first * per_chunk, tile_n, halo_q, 0)
    send_out(out_q, qg_hbm, top)

    if whole_sum:
        for copy in ss_copies:
            copy.wait_recv()
        ss = jnp.sum(jnp.sum(squares[...], axis=0), keepdims=True)
        count = F32(raw.shape[0] * grp_n * LANES)
        factor = jnp.minimum(F32(1.0), jnp.sqrt(count / ss))
        fg_ref[...] = gathered[...] * factor
        for copy in rs_copies + ag_copies + ss_copies:
            copy.wait_send()

    @pl.when(has_left)
    def _():
        for chunk in range(chunk_n):
            dz_copy(chunk).wait_send()

    @pl.when(has_right)
    def _():
        for chunk in range(chunk_n):
            u_copy(chunk).wait_send()

    for copy in out_copies:
        copy.wait()


def on_device(seq_n, grp_n, query_proj, key_proj, value_proj, out_grad, filters):
    rows, chan = query_proj.shape
    group_n, tap_n = filters.shape
    assert tap_n == LANES and rows == 2 * LANES and chan == group_n * GSIZE
    tile_n = chan // LANES
    chunk_n = 4 if tile_n % 4 == 0 else 1
    whole_sum = group_n % (8 * seq_n) == 0
    own = group_n // seq_n if whole_sum else 8
    dense = jax.ShapeDtypeStruct((rows, chan), BF16)
    anywhere = pl.BlockSpec(memory_space=pl.ANY)
    vmem = pl.BlockSpec(memory_space=pltpu.VMEM)
    flat = pltpu.VMEM((rows, chan), BF16)
    dma = pltpu.SemaphoreType.DMA
    query_grad, key_grad, value_grad, sums = pl.pallas_call(
        functools.partial(kernel, seq_n, grp_n, whole_sum, chunk_n),
        out_shape=(dense, dense, dense, jax.ShapeDtypeStruct((group_n, tap_n), F32)),
        in_specs=[anywhere] * 4 + [vmem],
        out_specs=(anywhere, anywhere, anywhere, vmem),
        scratch_shapes=[flat] * 4
        + [pltpu.VMEM((tile_n, rows, LANES), BF16)] * 2
        + [pltpu.VMEM((tile_n, LANES, LANES), BF16)] * 2
        + [pltpu.VMEM((tile_n, PER_TILE * LANES, 2 * LANES), BF16)] * 2
        + [flat] * 3
        + [
            pltpu.VMEM((2, group_n, LANES), F32),
            pltpu.VMEM((group_n, LANES), F32),
            pltpu.VMEM((seq_n, own, LANES), F32),
            pltpu.VMEM((group_n, LANES), F32),
            pltpu.VMEM((grp_n, 8, LANES), F32),
            dma((8,)), dma((6,)), dma((2, chunk_n)), dma((2, chunk_n)),
            dma((seq_n,)), dma((seq_n,)), dma((seq_n,)), dma((seq_n,)),
            dma((grp_n,)), dma((grp_n,)),
        ],
        compiler_params=pltpu.CompilerParams(
            collective_id=0, has_side_effects=True, vmem_limit_bytes=48 * 1024 * 1024
        ),
        cost_estimate=pl.CostEstimate(
            flops=12 * rows * chan * LANES * PER_TILE, bytes_accessed=14 * rows * chan, transcendentals=0
        ),
    )(query_proj, key_proj, value_proj, out_grad, filters)
    if whole_sum:
        return query_grad, key_grad, value_grad, sums
    sums = lax.psum(sums, "seq")
    squares = lax.psum(jnp.sum(sums * sums), "grp")
    factor = jnp.minimum(F32(1.0), jnp.sqrt(F32(group_n * grp_n * tap_n) / squares))
    return query_grad, key_grad, value_grad, sums * factor


def solution(mesh):
    split = P("seq", "grp")
    return jax.shard_map(
        functools.partial(on_device, mesh.shape["seq"], mesh.shape["grp"]),
        mesh=mesh,
        in_specs=(split, split, split, split, P("grp", None)),
        out_specs=(split, split, split, P("grp", None)),
        check_vma=False,
    )
```

```python
import functools

import jax
import jax.numpy as jnp
from jax import lax
from jax.experimental import pallas as pl
from jax.experimental.pallas import tpu as pltpu
from jax.sharding import PartitionSpec as P

GSIZE = 16
LANES = 128
PER_TILE = LANES // GSIZE
CORR_BATCH = 8
UNROLL = 2
MESH = pl.DeviceIdType.MESH
F32 = jnp.float32
BF16 = jnp.bfloat16


def product(a, b):
    return (a.astype(F32) * b.astype(F32)).astype(BF16)


def kernel(
    seq_n, grp_n, whole_sum, chunk_n,
    q_hbm, k_hbm, v_hbm, g_hbm, h_ref,
    qg_hbm, kg_hbm, vg_hbm, fg_ref,
    q, k, v, g, u, dz, u_halo, dz_halo, fmat, bmat, out_q, out_k, out_v,
    taps, raw, scattered, gathered, squares,
    in_sem, out_sem, halo_send, halo_recv, rs_send, rs_recv, ag_send, ag_recv, ss_send, ss_recv,
):
    me, mine = lax.axis_index("seq"), lax.axis_index("grp")
    tile_n = u.shape[0]
    half = LANES
    top, low = pl.ds(0, half), pl.ds(half, half)
    per_chunk = tile_n // chunk_n

    loads = []
    order = ((g_hbm, g, top), (q_hbm, q, top), (k_hbm, k, low), (v_hbm, v, low),
             (g_hbm, g, low), (q_hbm, q, low), (k_hbm, k, top), (v_hbm, v, top))
    for index, (source, target, rows) in enumerate(order):
        copy = pltpu.make_async_copy(source.at[rows], target.at[rows], in_sem.at[index])
        copy.start()
        loads.append(copy)

    def at_seq(position):
        return {"seq": position, "grp": mine}

    def at_grp(position):
        return {"seq": me, "grp": position}

    seq_peers = [lax.rem(me + step, seq_n) for step in range(1, seq_n)] if whole_sum else []
    grp_peers = [lax.rem(mine + step, grp_n) for step in range(1, grp_n)] if whole_sum else []
    has_left, has_right = me > 0, me < seq_n - 1
    barrier = pltpu.get_barrier_semaphore()
    if whole_sum:
        for peer in seq_peers:
            pl.semaphore_signal(barrier, 1, device_id=at_seq(peer), device_id_type=MESH)
        for peer in grp_peers:
            pl.semaphore_signal(barrier, 1, device_id=at_grp(peer), device_id_type=MESH)
    else:
        @pl.when(has_left)
        def _():
            pl.semaphore_signal(barrier, 1, device_id=at_seq(me - 1), device_id_type=MESH)

        @pl.when(has_right)
        def _():
            pl.semaphore_signal(barrier, 1, device_id=at_seq(me + 1), device_id_type=MESH)

    h = h_ref[...]
    row = lax.broadcasted_iota(jnp.int32, (half, half), 0)
    col = lax.broadcasted_iota(jnp.int32, (half, half), 1)
    flip = (((row + col) == 0) | ((row + col) == half)).astype(BF16)
    taps[0] = h.astype(F32)
    taps[1] = jnp.dot(h, flip, preferred_element_type=F32)

    @pl.when(jnp.logical_not(has_left))
    def _():
        u_halo[...] = jnp.zeros_like(u_halo)

    @pl.when(jnp.logical_not(has_right))
    def _():
        dz_halo[...] = jnp.zeros_like(dz_halo)

    def cols(tile):
        return pl.ds(pl.multiple_of(tile * LANES, LANES), LANES)

    def dz_copy(chunk):
        tiles = pl.ds(chunk * per_chunk, per_chunk)
        return pltpu.make_async_remote_copy(
            src_ref=dz.at[tiles, top], dst_ref=dz_halo.at[tiles],
            send_sem=halo_send.at[0, chunk], recv_sem=halo_recv.at[0, chunk],
            device_id=at_seq(me - 1), device_id_type=MESH)

    def u_copy(chunk):
        tiles = pl.ds(chunk * per_chunk, per_chunk)
        return pltpu.make_async_remote_copy(
            src_ref=u.at[tiles, low], dst_ref=u_halo.at[tiles],
            send_sem=halo_send.at[1, chunk], recv_sem=halo_recv.at[1, chunk],
            device_id=at_seq(me + 1), device_id_type=MESH)

    loads[0].wait()
    loads[1].wait()
    for tile in range(tile_n):
        dz[tile, top] = product(g[top, cols(tile)], q[top, cols(tile)])
    loads[2].wait()
    loads[3].wait()
    for tile in range(tile_n):
        u[tile, low] = product(k[low, cols(tile)], v[low, cols(tile)])

    if whole_sum:
        pl.semaphore_wait(barrier, seq_n + grp_n - 2)
    else:
        @pl.when(has_left)
        def _():
            pl.semaphore_wait(barrier, 1)

        @pl.when(has_right)
        def _():
            pl.semaphore_wait(barrier, 1)

    @pl.when(has_left)
    def _():
        for chunk in range(chunk_n):
            dz_copy(chunk).start()

    for index in range(4, 8):
        loads[index].wait()
    for tile in range(tile_n):
        dz[tile, low] = product(g[low, cols(tile)], q[low, cols(tile)])
        u[tile, top] = product(k[top, cols(tile)], v[top, cols(tile)])

    lane_group = lax.broadcasted_iota(jnp.int32, (half, LANES), 1) // GSIZE

    def pick(stacked):
        out = stacked[0:half]
        for member in range(1, PER_TILE):
            out = jnp.where(lane_group == member, stacked[member * half:(member + 1) * half], out)
        return out

    def conv(table, tile, pair):
        return pick(jnp.dot(table[tile], pair, preferred_element_type=F32))

    def store_q(tile, rows, z):
        out_q[rows, cols(tile)] = (g[rows, cols(tile)].astype(F32) * z).astype(BF16)

    def store_kv(tile, rows, du):
        out_k[rows, cols(tile)] = (v[rows, cols(tile)].astype(F32) * du).astype(BF16)
        out_v[rows, cols(tile)] = (k[rows, cols(tile)].astype(F32) * du).astype(BF16)

    def local_part(tile, carry):
        base = pl.multiple_of(tile * PER_TILE, PER_TILE)
        plain = taps[0, pl.ds(base, PER_TILE), :]
        turned = taps[1, pl.ds(base, PER_TILE), :]
        for member in range(PER_TILE):
            rows = pl.ds(member * half, half)
            spread = jnp.broadcast_to(plain[member:member + 1], (half, half))
            circ = pltpu.roll(spread, 0, 1, stride=1, stride_axis=0)
            bmat[tile, rows, 0:half] = jnp.where(col >= row, circ, 0.0).astype(BF16)
            bmat[tile, rows, half:2 * half] = jnp.where(col < row, circ, 0.0).astype(BF16)
            spread = jnp.broadcast_to(turned[member:member + 1], (half, half))
            circ = pltpu.roll(spread, 0, 1, stride=1, stride_axis=0)
            fmat[tile, rows, 0:half] = jnp.where(col > row, circ, 0.0).astype(BF16)
            fmat[tile, rows, half:2 * half] = jnp.where(col <= row, circ, 0.0).astype(BF16)
        store_q(tile, low, conv(fmat, tile, u[tile]))
        store_kv(tile, top, conv(bmat, tile, dz[tile]))
        return carry

    early = max(1, tile_n // 2)
    lax.fori_loop(0, early, local_part, 0, unroll=UNROLL)

    @pl.when(has_left)
    def _():
        for chunk in range(chunk_n):
            dz_copy(chunk).wait_send()


    lax.fori_loop(early, tile_n, local_part, 0, unroll=UNROLL)

    out_copies = []

    def send_out(source, target, rows):
        copy = pltpu.make_async_copy(source.at[rows], target.at[rows], out_sem.at[len(out_copies)])
        copy.start()
        out_copies.append(copy)

    send_out(out_q, qg_hbm, low)
    send_out(out_k, kg_hbm, top)
    send_out(out_v, vg_hbm, top)

    sub = lax.broadcasted_iota(jnp.int32, (PER_TILE, 8, LANES), 1)
    lanes256 = lax.broadcasted_iota(jnp.int32, (half, 2 * LANES), 1) % LANES // GSIZE

    def correlate(tile, carry):
        both = jnp.concatenate([u[tile, top], u[tile, low]], axis=1)
        window = jnp.concatenate(
            [jnp.concatenate([dz[tile, top], dz[tile, low]], axis=1),
             jnp.concatenate([dz[tile, low], dz_halo[tile]], axis=1)], axis=0)
        parts = []
        for start in range(0, PER_TILE, CORR_BATCH):
            members = range(start, start + CORR_BATCH)
            left = jnp.concatenate(
                [jnp.where(lanes256 == member, both, jnp.zeros_like(both)) for member in members], axis=0)
            c = lax.dot_general(left, window, (((1,), (1,)), ((), ())), preferred_element_type=F32)
            for place in range(CORR_BATCH):
                rows = slice(place * half, (place + 1) * half)
                m = jnp.where(col >= row, c[rows, :half], c[rows, half:])
                size = half // 2
                while size >= 8:
                    m = m[:size] + pltpu.roll(m[size:], LANES - size, 1)
                    size //= 2
                parts.append(m.reshape(1, 8, LANES))
        folded = jnp.concatenate(parts, axis=0)
        for bit in (1, 2, 4):
            folded = jnp.where((sub & bit) != 0, pltpu.roll(folded, LANES - bit, 2), folded)
        raw[pl.ds(pl.multiple_of(tile * PER_TILE, PER_TILE), PER_TILE), :] = jnp.sum(folded, axis=1)
        return carry

    for chunk in range(chunk_n):
        @pl.when(has_right)
        def _():
            dz_copy(chunk).wait_recv()

        lax.fori_loop(chunk * per_chunk, (chunk + 1) * per_chunk, correlate, 0, unroll=UNROLL)

    if whole_sum:
        own = raw.shape[0] // seq_n
        my_rows = pl.ds(pl.multiple_of(me * own, own), own)
        rs_copies, ag_copies, ss_copies = [], [], []
        for step, peer in enumerate(seq_peers):
            rs_copies.append(pltpu.make_async_remote_copy(
                src_ref=raw.at[pl.ds(pl.multiple_of(peer * own, own), own)],
                dst_ref=scattered.at[step], send_sem=rs_send.at[step], recv_sem=rs_recv.at[step],
                device_id=at_seq(peer), device_id_type=MESH))
            rs_copies[-1].start()
    else:
        fg_ref[...] = raw[...]

    @pl.when(has_right)
    def _():
        for chunk in range(chunk_n):
            u_copy(chunk).start()

    def halo_q(tile, carry):
        pair = jnp.concatenate([u_halo[tile], u[tile, top]], axis=0)
        store_q(tile, top, conv(fmat, tile, pair))
        return carry

    def halo_kv(tile, carry):
        pair = jnp.concatenate([dz[tile, low], dz_halo[tile]], axis=0)
        store_kv(tile, low, conv(bmat, tile, pair))
        return carry

    lax.fori_loop(0, tile_n, halo_kv, 0, unroll=UNROLL)
    send_out(out_k, kg_hbm, low)
    send_out(out_v, vg_hbm, low)

    if whole_sum:
        total = raw[my_rows]
        for step, copy in enumerate(rs_copies):
            copy.wait_recv()
            total = total + scattered[step]
        gathered[my_rows] = total
        for step, peer in enumerate(seq_peers):
            ag_copies.append(pltpu.make_async_remote_copy(
                src_ref=gathered.at[my_rows], dst_ref=gathered.at[my_rows],
                send_sem=ag_send.at[step], recv_sem=ag_recv.at[step],
                device_id=at_seq(peer), device_id_type=MESH))
            ag_copies[-1].start()

    first = max(1, chunk_n // 2)
    for chunk in range(first):
        @pl.when(has_left)
        def _():
            u_copy(chunk).wait_recv()

    lax.fori_loop(0, first * per_chunk, halo_q, 0, unroll=UNROLL)

    if whole_sum:
        for copy in ag_copies:
            copy.wait_recv()
        values = gathered[...]
        part = jnp.sum((values * values).reshape(-1, 8, LANES), axis=0)
        squares[0] = part
        for step, peer in enumerate(grp_peers):
            ss_copies.append(pltpu.make_async_remote_copy(
                src_ref=squares.at[0], dst_ref=squares.at[step + 1],
                send_sem=ss_send.at[step], recv_sem=ss_recv.at[step],
                device_id=at_grp(peer), device_id_type=MESH))
            ss_copies[-1].start()

    for chunk in range(first, chunk_n):
        @pl.when(has_left)
        def _():
            u_copy(chunk).wait_recv()

    lax.fori_loop(first * per_chunk, tile_n, halo_q, 0, unroll=UNROLL)
    send_out(out_q, qg_hbm, top)

    if whole_sum:
        for copy in ss_copies:
            copy.wait_recv()
        ss = jnp.sum(jnp.sum(squares[...], axis=0), keepdims=True)
        count = F32(raw.shape[0] * grp_n * LANES)
        factor = jnp.minimum(F32(1.0), jnp.sqrt(count / ss))
        fg_ref[...] = gathered[...] * factor
        for copy in rs_copies + ag_copies + ss_copies:
            copy.wait_send()

    @pl.when(has_right)
    def _():
        for chunk in range(chunk_n):
            u_copy(chunk).wait_send()

    for copy in out_copies:
        copy.wait()


def on_device(seq_n, grp_n, query_proj, key_proj, value_proj, out_grad, filters):
    rows, chan = query_proj.shape
    group_n, tap_n = filters.shape
    assert tap_n == LANES and rows == 2 * LANES and chan == group_n * GSIZE
    tile_n = chan // LANES
    chunk_n = 4 if tile_n % 4 == 0 else 1
    whole_sum = group_n % (8 * seq_n) == 0
    own = group_n // seq_n if whole_sum else 8
    dense = jax.ShapeDtypeStruct((rows, chan), BF16)
    anywhere = pl.BlockSpec(memory_space=pl.ANY)
    vmem = pl.BlockSpec(memory_space=pltpu.VMEM)
    flat = pltpu.VMEM((rows, chan), BF16)
    dma = pltpu.SemaphoreType.DMA
    query_grad, key_grad, value_grad, sums = pl.pallas_call(
        functools.partial(kernel, seq_n, grp_n, whole_sum, chunk_n),
        out_shape=(dense, dense, dense, jax.ShapeDtypeStruct((group_n, tap_n), F32)),
        in_specs=[anywhere] * 4 + [vmem],
        out_specs=(anywhere, anywhere, anywhere, vmem),
        scratch_shapes=[flat] * 4
        + [pltpu.VMEM((tile_n, rows, LANES), BF16)] * 2
        + [pltpu.VMEM((tile_n, LANES, LANES), BF16)] * 2
        + [pltpu.VMEM((tile_n, PER_TILE * LANES, 2 * LANES), BF16)] * 2
        + [flat] * 3
        + [
            pltpu.VMEM((2, group_n, LANES), F32),
            pltpu.VMEM((group_n, LANES), F32),
            pltpu.VMEM((seq_n, own, LANES), F32),
            pltpu.VMEM((group_n, LANES), F32),
            pltpu.VMEM((grp_n, 8, LANES), F32),
            dma((8,)), dma((6,)), dma((2, chunk_n)), dma((2, chunk_n)),
            dma((seq_n,)), dma((seq_n,)), dma((seq_n,)), dma((seq_n,)),
            dma((grp_n,)), dma((grp_n,)),
        ],
        compiler_params=pltpu.CompilerParams(
            collective_id=0, has_side_effects=True, vmem_limit_bytes=60 * 1024 * 1024
        ),
        cost_estimate=pl.CostEstimate(
            flops=12 * rows * chan * LANES * PER_TILE, bytes_accessed=14 * rows * chan, transcendentals=0
        ),
    )(query_proj, key_proj, value_proj, out_grad, filters)
    if whole_sum:
        return query_grad, key_grad, value_grad, sums
    sums = lax.psum(sums, "seq")
    squares = lax.psum(jnp.sum(sums * sums), "grp")
    factor = jnp.minimum(F32(1.0), jnp.sqrt(F32(group_n * grp_n * tap_n) / squares))
    return query_grad, key_grad, value_grad, sums * factor


def solution(mesh):
    split = P("seq", "grp")
    return jax.shard_map(
        functools.partial(on_device, mesh.shape["seq"], mesh.shape["grp"]),
        mesh=mesh,
        in_specs=(split, split, split, split, P("grp", None)),
        out_specs=(split, split, split, P("grp", None)),
        check_vma=False,
    )
```

```python
import functools

import jax
import jax.numpy as jnp
from jax import lax
from jax.experimental import pallas as pl
from jax.experimental.pallas import tpu as pltpu
from jax.sharding import PartitionSpec as P

GSIZE = 16
LANES = 128
PER_TILE = LANES // GSIZE
CORR_BATCH = 8
UNROLL = 2
MESH = pl.DeviceIdType.MESH
F32 = jnp.float32
BF16 = jnp.bfloat16


def product(a, b):
    return (a.astype(F32) * b.astype(F32)).astype(BF16)


def kernel(
    seq_n, grp_n, whole_sum, chunk_n,
    q_hbm, k_hbm, v_hbm, g_hbm, h_hbm,
    qg_hbm, kg_hbm, vg_hbm, fg_ref,
    q, k, v, g, h_own, u, dz, u_halo, dz_halo, fmat, bmat, out_q, out_k, out_v,
    taps, raw, scattered, gathered, squares, own_square,
    in_sem, out_sem, halo_send, halo_recv, rs_send, rs_recv, ag_send, ag_recv, ss_send, ss_recv,
):
    me, mine = lax.axis_index("seq"), lax.axis_index("grp")
    tile_n = u.shape[0]
    half = LANES
    top, low = pl.ds(0, half), pl.ds(half, half)
    per_chunk = tile_n // chunk_n

    loads = []
    order = ((g_hbm, g, top), (q_hbm, q, top), (k_hbm, k, low), (v_hbm, v, low),
             (g_hbm, g, low), (q_hbm, q, low), (k_hbm, k, top), (v_hbm, v, top))
    for index, (source, target, rows) in enumerate(order):
        copy = pltpu.make_async_copy(source.at[rows], target.at[rows], in_sem.at[index])
        copy.start()
        loads.append(copy)
    load_h = pltpu.make_async_copy(h_hbm, h_own, in_sem.at[len(order)])
    load_h.start()

    def at_seq(position):
        return {"seq": position, "grp": mine}

    def at(seq_at, grp_at):
        return {"seq": seq_at, "grp": grp_at}

    seq_peers = [lax.rem(me + step, seq_n) for step in range(1, seq_n)] if whole_sum else []
    far_peers = [
        (lax.rem(me + seq_step, seq_n), lax.rem(mine + grp_step, grp_n))
        for grp_step in range(1, grp_n) for seq_step in range(seq_n)
    ] if whole_sum else []
    has_left, has_right = me > 0, me < seq_n - 1
    barrier = pltpu.get_barrier_semaphore()
    if whole_sum:
        for peer in seq_peers:
            pl.semaphore_signal(barrier, 1, device_id=at_seq(peer), device_id_type=MESH)
        for peer in far_peers:
            pl.semaphore_signal(barrier, 1, device_id=at(*peer), device_id_type=MESH)
    else:
        @pl.when(has_left)
        def _():
            pl.semaphore_signal(barrier, 1, device_id=at_seq(me - 1), device_id_type=MESH)

        @pl.when(has_right)
        def _():
            pl.semaphore_signal(barrier, 1, device_id=at_seq(me + 1), device_id_type=MESH)

    @pl.when(jnp.logical_not(has_left))
    def _():
        u_halo[...] = jnp.zeros_like(u_halo)

    @pl.when(jnp.logical_not(has_right))
    def _():
        dz_halo[...] = jnp.zeros_like(dz_halo)

    def cols(tile):
        return pl.ds(pl.multiple_of(tile * LANES, LANES), LANES)

    def dz_copy(chunk):
        tiles = pl.ds(chunk * per_chunk, per_chunk)
        return pltpu.make_async_remote_copy(
            src_ref=dz.at[tiles, top], dst_ref=dz_halo.at[tiles],
            send_sem=halo_send.at[0, chunk], recv_sem=halo_recv.at[0, chunk],
            device_id=at_seq(me - 1), device_id_type=MESH)

    def u_copy(chunk):
        tiles = pl.ds(chunk * per_chunk, per_chunk)
        return pltpu.make_async_remote_copy(
            src_ref=u.at[tiles, low], dst_ref=u_halo.at[tiles],
            send_sem=halo_send.at[1, chunk], recv_sem=halo_recv.at[1, chunk],
            device_id=at_seq(me + 1), device_id_type=MESH)

    loads[0].wait()
    loads[1].wait()
    for tile in range(tile_n):
        dz[tile, top] = product(g[top, cols(tile)], q[top, cols(tile)])
    if whole_sum:
        pl.semaphore_wait(barrier, seq_n * grp_n - 1)
    else:
        @pl.when(has_left)
        def _():
            pl.semaphore_wait(barrier, 1)

        @pl.when(has_right)
        def _():
            pl.semaphore_wait(barrier, 1)

    @pl.when(has_left)
    def _():
        for chunk in range(chunk_n):
            dz_copy(chunk).start()

    loads[2].wait()
    loads[3].wait()
    for tile in range(tile_n):
        u[tile, low] = product(k[low, cols(tile)], v[low, cols(tile)])

    for index in range(4, 8):
        loads[index].wait()
    for tile in range(tile_n):
        dz[tile, low] = product(g[low, cols(tile)], q[low, cols(tile)])
        u[tile, top] = product(k[top, cols(tile)], v[top, cols(tile)])

    load_h.wait()
    h = h_own[...]
    row = lax.broadcasted_iota(jnp.int32, (half, half), 0)
    col = lax.broadcasted_iota(jnp.int32, (half, half), 1)
    flip = (((row + col) == 0) | ((row + col) == half)).astype(BF16)
    taps[0] = h.astype(F32)
    taps[1] = jnp.dot(h, flip, preferred_element_type=F32)

    lane_group = lax.broadcasted_iota(jnp.int32, (half, LANES), 1) // GSIZE

    def pick(stacked):
        out = stacked[0:half]
        for member in range(1, PER_TILE):
            out = jnp.where(lane_group == member, stacked[member * half:(member + 1) * half], out)
        return out

    def conv(table, tile, pair):
        return pick(jnp.dot(table[tile], pair, preferred_element_type=F32))

    def store_q(tile, rows, z):
        out_q[rows, cols(tile)] = (g[rows, cols(tile)].astype(F32) * z).astype(BF16)

    def store_kv(tile, rows, du):
        out_k[rows, cols(tile)] = (v[rows, cols(tile)].astype(F32) * du).astype(BF16)
        out_v[rows, cols(tile)] = (k[rows, cols(tile)].astype(F32) * du).astype(BF16)

    def local_part(tile, carry):
        base = pl.multiple_of(tile * PER_TILE, PER_TILE)
        plain = taps[0, pl.ds(base, PER_TILE), :]
        turned = taps[1, pl.ds(base, PER_TILE), :]
        for member in range(PER_TILE):
            rows = pl.ds(member * half, half)
            spread = jnp.broadcast_to(plain[member:member + 1], (half, half))
            circ = pltpu.roll(spread, 0, 1, stride=1, stride_axis=0)
            bmat[tile, rows, 0:half] = jnp.where(col >= row, circ, 0.0).astype(BF16)
            bmat[tile, rows, half:2 * half] = jnp.where(col < row, circ, 0.0).astype(BF16)
            spread = jnp.broadcast_to(turned[member:member + 1], (half, half))
            circ = pltpu.roll(spread, 0, 1, stride=1, stride_axis=0)
            fmat[tile, rows, 0:half] = jnp.where(col > row, circ, 0.0).astype(BF16)
            fmat[tile, rows, half:2 * half] = jnp.where(col <= row, circ, 0.0).astype(BF16)
        store_q(tile, low, conv(fmat, tile, u[tile]))
        store_kv(tile, top, conv(bmat, tile, dz[tile]))
        return carry

    early = max(1, tile_n // 2)
    lax.fori_loop(0, early, local_part, 0, unroll=UNROLL)

    @pl.when(has_left)
    def _():
        for chunk in range(chunk_n):
            dz_copy(chunk).wait_send()


    lax.fori_loop(early, tile_n, local_part, 0, unroll=UNROLL)

    out_copies = []

    def send_out(source, target, rows):
        copy = pltpu.make_async_copy(source.at[rows], target.at[rows], out_sem.at[len(out_copies)])
        copy.start()
        out_copies.append(copy)

    send_out(out_q, qg_hbm, low)
    send_out(out_k, kg_hbm, top)
    send_out(out_v, vg_hbm, top)

    sub = lax.broadcasted_iota(jnp.int32, (PER_TILE, 8, LANES), 1)
    lanes256 = lax.broadcasted_iota(jnp.int32, (half, 2 * LANES), 1) % LANES // GSIZE

    def correlate(tile, carry):
        both = jnp.concatenate([u[tile, top], u[tile, low]], axis=1)
        window = jnp.concatenate(
            [jnp.concatenate([dz[tile, top], dz[tile, low]], axis=1),
             jnp.concatenate([dz[tile, low], dz_halo[tile]], axis=1)], axis=0)
        parts = []
        for start in range(0, PER_TILE, CORR_BATCH):
            members = range(start, start + CORR_BATCH)
            left = jnp.concatenate(
                [jnp.where(lanes256 == member, both, jnp.zeros_like(both)) for member in members], axis=0)
            c = lax.dot_general(left, window, (((1,), (1,)), ((), ())), preferred_element_type=F32)
            for place in range(CORR_BATCH):
                rows = slice(place * half, (place + 1) * half)
                m = jnp.where(col >= row, c[rows, :half], c[rows, half:])
                size = half // 2
                while size >= 8:
                    m = m[:size] + pltpu.roll(m[size:], LANES - size, 1)
                    size //= 2
                parts.append(m.reshape(1, 8, LANES))
        folded = jnp.concatenate(parts, axis=0)
        for bit in (1, 2, 4):
            folded = jnp.where((sub & bit) != 0, pltpu.roll(folded, LANES - bit, 2), folded)
        raw[pl.ds(pl.multiple_of(tile * PER_TILE, PER_TILE), PER_TILE), :] = jnp.sum(folded, axis=1)
        return carry

    for chunk in range(chunk_n):
        @pl.when(has_right)
        def _():
            dz_copy(chunk).wait_recv()

        lax.fori_loop(chunk * per_chunk, (chunk + 1) * per_chunk, correlate, 0, unroll=UNROLL)

    if whole_sum:
        own = raw.shape[0] // seq_n
        my_rows = pl.ds(pl.multiple_of(me * own, own), own)
        rs_copies, ag_copies, ss_copies = [], [], []
        for step, peer in enumerate(seq_peers):
            rs_copies.append(pltpu.make_async_remote_copy(
                src_ref=raw.at[pl.ds(pl.multiple_of(peer * own, own), own)],
                dst_ref=scattered.at[step], send_sem=rs_send.at[step], recv_sem=rs_recv.at[step],
                device_id=at_seq(peer), device_id_type=MESH))
            rs_copies[-1].start()
    else:
        fg_ref[...] = raw[...]

    @pl.when(has_right)
    def _():
        for chunk in range(chunk_n):
            u_copy(chunk).start()

    def halo_q(tile, carry):
        pair = jnp.concatenate([u_halo[tile], u[tile, top]], axis=0)
        store_q(tile, top, conv(fmat, tile, pair))
        return carry

    def halo_kv(tile, carry):
        pair = jnp.concatenate([dz[tile, low], dz_halo[tile]], axis=0)
        store_kv(tile, low, conv(bmat, tile, pair))
        return carry

    lax.fori_loop(0, tile_n, halo_kv, 0, unroll=UNROLL)
    send_out(out_k, kg_hbm, low)
    send_out(out_v, vg_hbm, low)

    if whole_sum:
        total = raw[my_rows]
        for step, copy in enumerate(rs_copies):
            copy.wait_recv()
            total = total + scattered[step]
        gathered[my_rows] = total
        own_square[...] = jnp.sum(total * total, axis=0, keepdims=True)
        for step, peer in enumerate(seq_peers):
            ag_copies.append(pltpu.make_async_remote_copy(
                src_ref=gathered.at[my_rows], dst_ref=gathered.at[my_rows],
                send_sem=ag_send.at[step], recv_sem=ag_recv.at[step],
                device_id=at_seq(peer), device_id_type=MESH))
            ag_copies[-1].start()
        for slot, peer in enumerate(far_peers):
            ss_copies.append(pltpu.make_async_remote_copy(
                src_ref=own_square, dst_ref=squares.at[pl.ds(slot, 1)],
                send_sem=ss_send.at[slot], recv_sem=ss_recv.at[slot],
                device_id=at(*peer), device_id_type=MESH))
            ss_copies[-1].start()

    for chunk in range(chunk_n):
        @pl.when(has_left)
        def _():
            u_copy(chunk).wait_recv()

        lax.fori_loop(chunk * per_chunk, (chunk + 1) * per_chunk, halo_q, 0, unroll=UNROLL)

    send_out(out_q, qg_hbm, top)

    if whole_sum:
        for copy in ag_copies + ss_copies:
            copy.wait_recv()
        values = gathered[...]
        ss = jnp.sum(values * values, keepdims=True)
        if far_peers:
            ss = ss + jnp.sum(squares[...], keepdims=True)
        count = F32(raw.shape[0] * grp_n * LANES)
        factor = jnp.minimum(F32(1.0), jnp.sqrt(count / ss))
        fg_ref[...] = values * factor
        for copy in rs_copies + ag_copies + ss_copies:
            copy.wait_send()

    @pl.when(has_right)
    def _():
        for chunk in range(chunk_n):
            u_copy(chunk).wait_send()

    for copy in out_copies:
        copy.wait()


def on_device(seq_n, grp_n, query_proj, key_proj, value_proj, out_grad, filters):
    rows, chan = query_proj.shape
    group_n, tap_n = filters.shape
    assert tap_n == LANES and rows == 2 * LANES and chan == group_n * GSIZE
    tile_n = chan // LANES
    chunk_n = 4 if tile_n % 4 == 0 else 1
    whole_sum = group_n % (8 * seq_n) == 0
    far_n = max(1, (grp_n - 1) * seq_n)
    own = group_n // seq_n if whole_sum else 8
    dense = jax.ShapeDtypeStruct((rows, chan), BF16)
    anywhere = pl.BlockSpec(memory_space=pl.ANY)
    vmem = pl.BlockSpec(memory_space=pltpu.VMEM)
    flat = pltpu.VMEM((rows, chan), BF16)
    dma = pltpu.SemaphoreType.DMA
    query_grad, key_grad, value_grad, sums = pl.pallas_call(
        functools.partial(kernel, seq_n, grp_n, whole_sum, chunk_n),
        out_shape=(dense, dense, dense, jax.ShapeDtypeStruct((group_n, tap_n), F32)),
        in_specs=[anywhere] * 5,
        out_specs=(anywhere, anywhere, anywhere, vmem),
        scratch_shapes=[flat] * 4
        + [pltpu.VMEM((group_n, tap_n), BF16)]
        + [pltpu.VMEM((tile_n, rows, LANES), BF16)] * 2
        + [pltpu.VMEM((tile_n, LANES, LANES), BF16)] * 2
        + [pltpu.VMEM((tile_n, PER_TILE * LANES, 2 * LANES), BF16)] * 2
        + [flat] * 3
        + [
            pltpu.VMEM((2, group_n, LANES), F32),
            pltpu.VMEM((group_n, LANES), F32),
            pltpu.VMEM((seq_n, own, LANES), F32),
            pltpu.VMEM((group_n, LANES), F32),
            pltpu.VMEM((far_n, LANES), F32),
            pltpu.VMEM((1, LANES), F32),
            dma((9,)), dma((6,)), dma((2, chunk_n)), dma((2, chunk_n)),
            dma((seq_n,)), dma((seq_n,)), dma((seq_n,)), dma((seq_n,)),
            dma((far_n,)), dma((far_n,)),
        ],
        compiler_params=pltpu.CompilerParams(
            collective_id=0, has_side_effects=True, vmem_limit_bytes=60 * 1024 * 1024
        ),
        cost_estimate=pl.CostEstimate(
            flops=12 * rows * chan * LANES * PER_TILE, bytes_accessed=14 * rows * chan, transcendentals=0
        ),
    )(query_proj, key_proj, value_proj, out_grad, filters)
    if whole_sum:
        return query_grad, key_grad, value_grad, sums
    sums = lax.psum(sums, "seq")
    squares = lax.psum(jnp.sum(sums * sums), "grp")
    factor = jnp.minimum(F32(1.0), jnp.sqrt(F32(group_n * grp_n * tap_n) / squares))
    return query_grad, key_grad, value_grad, sums * factor


def solution(mesh):
    split = P("seq", "grp")
    return jax.shard_map(
        functools.partial(on_device, mesh.shape["seq"], mesh.shape["grp"]),
        mesh=mesh,
        in_specs=(split, split, split, split, P("grp", None)),
        out_specs=(split, split, split, P("grp", None)),
        check_vma=False,
    )
```
